32 devices in a mesh: groups: 2 (over y), gx: 4 (over z), gy: 4 (over x, core).
Axes of the slice: x: 2, y: 2, z: 4, core: 2. Of those that a mesh axis runs over, the one named last changes fastest.
Arguments:
- residual: bfloat16 [64, 8192], P(('groups', 'gx'), 'gy'), parts along dimension 0, may hold values from -50 to 50
- norm_gain: bfloat16 [8192], P('gy'), may hold values from 0.5 to 2
- qkv_weight: bfloat16 [8192, 4608], P('gy', 'gx'), may hold values from -0.0625 to 0.0625
- out_weight: bfloat16 [4096, 8192], P('gx', 'gy'), may hold values from -0.375 to 0.375
- gate_weight: bfloat16 [8192, 16384], P('gy', 'gx'), may hold values from -0.0625 to 0.0625
- up_weight: bfloat16 [8192, 16384], P('gy', 'gx'), may hold values from -0.0625 to 0.0625
- down_weight: bfloat16 [16384, 8192], P('gx', 'gy'), may hold values from -0.046875 to 0.046875
- cache_keys: bfloat16 [64, 512, 256], P(('groups', 'gx', 'gy')), parts along dimension 0, may hold values from -150 to 150
- cache_values: bfloat16 [64, 512, 256], P(('groups', 'gx', 'gy')), parts along dimension 0, may hold values from -6 to 6
- lengths: int32 [64], P(('groups', 'gx', 'gy')), parts along dimension 0, may hold values from 1 to 512, as said below
- positions: int32 [64], P(('groups', 'gx', 'gy')), parts along dimension 0, may hold values from 0 to 2047
Outputs:
- update: bfloat16 [64, 8192], P(('groups', 'gx'), 'gy'), parts along dimension 0
The draws below stay inside these ranges and needn't reach their ends.
There are 2 independent parts, one for each index of `groups`. The reference program is written for one: setup_inputs(seed, part) draws one part's arguments, and reference() takes and returns one part's arrays. A program takes and returns all parts, laid end to end along the dimension named above; an argument that names none is the same for every part. Nothing has to cross between parts.
Inputs may be any that keep to these rules, and one draw needn't show every extreme that they name: `lengths`: at least one row has exactly 512 valid slots.
All inputs are finite; a program needn't handle non-finite values.
Results may differ from the reference program's by a relative error of at most 0.012.
Values may be sent and summed in bfloat16 or wider, within the bound.
A program may use at most 128 MiB of HBM per device.

```python
import math
import jax
import jax.numpy as jnp
from jax import lax

D = 8192
HEADS = 16
DH = 256
FF = 16384
CTX = 512
B = 32
Q = 4096
QKV = 4608
BLOCKS = 4


def draw_residual(key, part):
    key = jax.random.fold_in(key, 11)
    first_key, second_key, third_key = jax.random.split(key, 3)
    row_scale = 0.3 * jnp.exp(jnp.log(10.0) * jax.random.uniform(second_key, (B, 1), jnp.float32))
    column_pos = jnp.arange(D, dtype=jnp.float32)[None, :] / D
    col_scale = 0.4 * jnp.exp(jnp.log(3.0) * column_pos + jnp.log(3.4) * jax.random.uniform(third_key, (1, D), jnp.float32))
    values = jnp.clip(jax.random.normal(first_key, (B, D), jnp.float32), -4.0, 4.0)
    return (values * row_scale * col_scale).astype(jnp.bfloat16)


def draw_cache_keys(key, part):
    key = jax.random.fold_in(key, 23)
    first_key = jax.random.fold_in(key, 0)
    values = jnp.clip(jax.random.normal(first_key, (B, CTX, DH), jnp.float32), -6.0, 6.0)
    return values.astype(jnp.bfloat16)


def draw_lengths(key, part):
    key = jax.random.fold_in(key, 37)
    first_key, second_key = jax.random.split(key, 2)
    drawn = jax.random.randint(first_key, (B,), 1, CTX + 1, jnp.int32)
    chosen = jax.random.randint(second_key, (), 0, B, jnp.int32)
    return jnp.where(jnp.arange(B, dtype=jnp.int32) == chosen, CTX, drawn).astype(jnp.int32)


def place_ends(array, own_key, smallest, largest):
    longest = array.shape.index(max(array.shape))
    spots = []
    for shift in (0, 1):
        where = [jax.random.randint(jax.random.fold_in(own_key, axis), (), 0, length) for axis, length in enumerate(array.shape)]
        where[longest] = (where[longest] + shift) % array.shape[longest]
        spots.append(tuple(where))
    return array.at[spots[0]].set(smallest).at[spots[1]].set(largest)


def shard_levels(own_key, shape, cuts, smallest, top_value):
    loudness, own = 1.0, jax.random.fold_in(own_key, 6)
    for axis_at, shards_of in cuts:
        heights = jnp.exp(jax.random.uniform(jax.random.fold_in(own, axis_at), (shards_of,), jnp.float32, smallest / len(cuts), top_value / len(cuts)))
        loudness = loudness * jnp.repeat(heights, shape[axis_at] // shards_of).reshape([-1 if axis == axis_at else 1 for axis in range(len(shape))])
    return loudness


def bell_draw(stream_key, extent, deviation, limit, shards=(), held_as=jnp.bfloat16):
    array = jax.random.normal(stream_key, extent, jnp.float32) * deviation
    if len(shards) > 0:
        array = shard_levels(stream_key, extent, shards, -0.22, 0.18) * array
    return jnp.clip(array, min=-limit, max=limit).astype(held_as)


def setup_inputs(seed: int = 0, part: int = 0) -> dict:
    splits = jax.random.split(jax.random.key(seed), 12)
    part_keys = jax.random.split(jax.random.fold_in(splits[11], part), 12)
    return {
        "residual": draw_residual(jax.random.fold_in(jax.random.fold_in(splits[11], part), 71), part),
        "norm_gain": jnp.clip(jnp.exp(math.log(2.0) - 1.3862944 * jax.random.uniform(splits[1], (D,), jnp.float32) ** shard_levels(splits[1], (D,), ((0, 4),), -0.2, 0.2)), 0.5, 2.0).astype(jnp.bfloat16),
        "qkv_weight": bell_draw(splits[2], (D, QKV), D ** -0.5, 0.0625, ((0, 4), (1, 4))),
        "out_weight": bell_draw(splits[3], (Q, D), DH ** -0.5, 0.375, ((0, 4), (1, 4))),
        "gate_weight": bell_draw(splits[4], (D, FF), D ** -0.5, 0.0625, ((0, 4), (1, 4))),
        "up_weight": bell_draw(splits[5], (D, FF), D ** -0.5, 0.0625, ((0, 4), (1, 4))),
        "down_weight": bell_draw(splits[6], (FF, D), FF ** -0.5, 0.046875, ((0, 4), (1, 4))),
        "cache_keys": draw_cache_keys(jax.random.fold_in(jax.random.fold_in(splits[11], part), 71), part),
        "cache_values": bell_draw(part_keys[8], (B, CTX, DH), 1.0, 6.0, ((0, 16),)),
        "lengths": draw_lengths(jax.random.fold_in(jax.random.fold_in(splits[11], part), 71), part),
        "positions": place_ends(jax.random.randint(part_keys[10], (B,), 0, 2048), jax.random.fold_in(part_keys[10], 1), 0, 2047).astype(jnp.int32),
    }


def angles(token_positions, head_width):
    half_width = head_width // 2
    frequency = jnp.exp(jnp.arange(half_width, dtype=jnp.float32) * (-2.0 * jnp.log(10000.0) / head_width))
    return token_positions.astype(jnp.float32)[:, None] * frequency[None, :]

def rotary(vectors, turn):
    half_width = vectors.shape[-1] // 2
    first_half = vectors[..., :half_width]
    second_half = vectors[..., half_width:]
    cosine = jnp.cos(turn)
    sine_part = jnp.sin(turn)
    return jnp.concatenate([first_half * cosine - second_half * sine_part, first_half * sine_part + second_half * cosine], axis=-1)

def attend_rows(joined, cached_keys, cached_values, valid_lengths, token_positions):
    row_count = joined.shape[0]
    query_width = HEADS * DH
    queries = joined[:, :query_width].astype(jnp.float32).reshape(row_count, HEADS, DH)
    new_key = joined[:, query_width:query_width + DH].astype(jnp.float32)
    new_value = joined[:, query_width + DH:].astype(jnp.float32)
    turn = angles(token_positions, DH)
    rotated_queries = rotary(queries, turn[:, None, :]).astype(jnp.bfloat16)
    rotated_key = rotary(new_key, turn).astype(jnp.bfloat16)
    score_scale = DH ** (-0.5)
    scores = jnp.einsum('rhd,rcd->rhc', rotated_queries.astype(jnp.float32), cached_keys.astype(jnp.float32)) * score_scale
    visible = jnp.arange(CTX, dtype=jnp.int32)[None, None, :] < valid_lengths[:, None, None]
    scores = jnp.where(visible, scores, -jnp.inf)
    own_score = jnp.einsum('rhd,rd->rh', rotated_queries.astype(jnp.float32), rotated_key.astype(jnp.float32)) * score_scale
    top_score = jnp.maximum(lax.optimization_barrier(jnp.max(scores, axis=2)), own_score)
    shifted = jnp.exp(scores - top_score[:, :, None])
    own_shifted = jnp.exp(own_score - top_score)
    denominator = lax.optimization_barrier(jnp.sum(shifted, axis=2)) + own_shifted
    softmax_weights = (shifted / denominator[:, :, None]).astype(jnp.bfloat16)
    own_weight = (own_shifted / denominator).astype(jnp.bfloat16)
    mixed = jnp.einsum('rhc,rcd->rhd', softmax_weights.astype(jnp.float32), cached_values.astype(jnp.float32))
    mixed = mixed + own_weight.astype(jnp.float32)[:, :, None] * new_value[:, None, :]
    return mixed.reshape(row_count, query_width).astype(jnp.bfloat16)

def reference(residual, norm_gain, qkv_weight, out_weight, gate_weight, up_weight, down_weight, cache_keys, cache_values, lengths, positions):
    widened = residual.astype(jnp.float32)
    totals = lax.optimization_barrier(jnp.sum(widened * widened, axis=1))
    normed = (widened * lax.rsqrt(totals / D + 1e-06)[:, None] * norm_gain.astype(jnp.float32)).astype(jnp.bfloat16)
    joined = jnp.dot(normed, qkv_weight, preferred_element_type=jnp.float32).astype(jnp.bfloat16)
    attended = attend_rows(joined, cache_keys, cache_values, lengths, positions)
    gate_sum = jnp.dot(normed, gate_weight, preferred_element_type=jnp.float32)
    up_sum = jnp.dot(normed, up_weight, preferred_element_type=jnp.float32)
    hidden = (jax.nn.silu(gate_sum) * up_sum).astype(jnp.bfloat16)
    query_block = Q // BLOCKS
    hidden_block = FF // BLOCKS

    def add_block(running, block_index):
        attn_block = lax.dynamic_slice_in_dim(attended, block_index * query_block, query_block, 1)
        out_block = lax.dynamic_slice_in_dim(out_weight, block_index * query_block, query_block, 0)
        unit_block = lax.dynamic_slice_in_dim(hidden, block_index * hidden_block, hidden_block, 1)
        down_block = lax.dynamic_slice_in_dim(down_weight, block_index * hidden_block, hidden_block, 0)
        block_term = jnp.dot(attn_block, out_block, preferred_element_type=jnp.float32)
        block_term = block_term + jnp.dot(unit_block, down_block, preferred_element_type=jnp.float32)
        rounded = lax.optimization_barrier(block_term.astype(jnp.bfloat16))
        return (running + rounded.astype(jnp.float32), None)
    start_sum = jnp.zeros((residual.shape[0], D), jnp.float32)
    summed, _ = lax.scan(add_block, start_sum, jnp.arange(BLOCKS, dtype=jnp.int32))
    return summed.astype(jnp.bfloat16)
```

```python
import functools

import jax
import jax.numpy as jnp
import numpy as np
from jax import lax
from jax.experimental import pallas as pl
from jax.experimental.pallas import tpu as pltpu
from jax.sharding import PartitionSpec as P

D = 8192
LANES = 128
MESH = pl.DeviceIdType.MESH


def angles(token_positions, head_width):
    half_width = head_width // 2
    frequency = jnp.exp(
        jnp.arange(half_width, dtype=jnp.float32) * (-2.0 * jnp.log(10000.0) / head_width)
    )
    return token_positions.astype(jnp.float32)[:, None] * frequency[None, :]


def rotary(vectors, turn):
    half_width = vectors.shape[-1] // 2
    first_half = vectors[..., :half_width]
    second_half = vectors[..., half_width:]
    cosine = jnp.cos(turn)
    sine_part = jnp.sin(turn)
    return jnp.concatenate(
        [
            first_half * cosine - second_half * sine_part,
            first_half * sine_part + second_half * cosine,
        ],
        axis=-1,
    )


def attend(joined, cached_keys, cached_values, valid_lengths, token_positions):
    row_count = joined.shape[0]
    head_width = cached_keys.shape[2]
    query_width = joined.shape[1] - 2 * head_width
    head_count = query_width // head_width
    queries = joined[:, :query_width].astype(jnp.float32).reshape(row_count, head_count, head_width)
    new_key = joined[:, query_width : query_width + head_width].astype(jnp.float32)
    new_value = joined[:, query_width + head_width :].astype(jnp.float32)
    turn = angles(token_positions, head_width)
    rotated_queries = rotary(queries, turn[:, None, :]).astype(jnp.bfloat16)
    rotated_key = rotary(new_key, turn).astype(jnp.bfloat16)
    score_scale = head_width ** (-0.5)
    scores = (
        jnp.einsum("rhd,rcd->rhc", rotated_queries, cached_keys, preferred_element_type=jnp.float32)
        * score_scale
    )
    visible = (
        jnp.arange(cached_keys.shape[1], dtype=jnp.int32)[None, None, :]
        < valid_lengths[:, None, None]
    )
    scores = jnp.where(visible, scores, -jnp.inf)
    own_score = (
        jnp.einsum("rhd,rd->rh", rotated_queries, rotated_key, preferred_element_type=jnp.float32)
        * score_scale
    )
    top_score = jnp.maximum(jnp.max(scores, axis=2), own_score)
    shifted = jnp.exp(scores - top_score[:, :, None])
    own_shifted = jnp.exp(own_score - top_score)
    denominator = jnp.sum(shifted, axis=2) + own_shifted
    softmax_weights = (shifted / denominator[:, :, None]).astype(jnp.bfloat16)
    own_weight = (own_shifted / denominator).astype(jnp.bfloat16)
    mixed = jnp.einsum(
        "rhc,rcd->rhd", softmax_weights, cached_values, preferred_element_type=jnp.float32
    )
    mixed = mixed + own_weight.astype(jnp.float32)[:, :, None] * new_value[:, None, :]
    return mixed.reshape(row_count, query_width).astype(jnp.bfloat16)


def collective_shards(
    residual,
    norm_gain,
    qkv_weight,
    out_weight,
    gate_weight,
    up_weight,
    down_weight,
    cache_keys,
    cache_values,
    lengths,
    positions,
):
    gain_wide = norm_gain.astype(jnp.float32)
    widened = residual.astype(jnp.float32)
    totals = lax.psum(jnp.sum(widened * widened, axis=1), "gy")
    scaled_rows = (widened * lax.rsqrt(totals / D + 1e-06)[:, None] * gain_wide).astype(
        jnp.bfloat16
    )
    normed = lax.all_gather(scaled_rows, "gx", axis=0, tiled=True)
    qkv_part = jnp.dot(normed, qkv_weight, preferred_element_type=jnp.float32)
    gate_part = jnp.dot(normed, gate_weight, preferred_element_type=jnp.float32)
    up_part = jnp.dot(normed, up_weight, preferred_element_type=jnp.float32)
    swapped = lax.all_to_all(qkv_part, "gx", split_axis=0, concat_axis=1, tiled=True)
    rows_qkv = lax.psum_scatter(swapped, "gy", scatter_dimension=0, tiled=True).astype(jnp.bfloat16)
    attended = attend(rows_qkv, cache_keys, cache_values, lengths, positions)
    grouped = lax.all_gather(attended, "gy", axis=0, tiled=True)
    heads_out = lax.all_to_all(grouped, "gx", split_axis=1, concat_axis=0, tiled=True)
    gate_sum, up_sum = lax.psum((gate_part, up_part), "gy")
    hidden = (jax.nn.silu(gate_sum) * up_sum).astype(jnp.bfloat16)
    block_term = jnp.dot(heads_out, out_weight, preferred_element_type=jnp.float32)
    return lax.psum_scatter(
        (block_term + jnp.dot(hidden, down_weight, preferred_element_type=jnp.float32)).astype(
            jnp.bfloat16
        ),
        "gx",
        scatter_dimension=0,
        tiled=True,
    )


def block_kernel(
    sizes,
    res_ref, gain_ref, freq_ref, qkv_hbm, out_hbm, gate_hbm, up_hbm, down_hbm, keys_hbm, vals_hbm,
    len_ref, pos_ref,
    y_ref,
    qkv_w, out_w, gate_w, up_w, down_w, keys_v, vals_v,
    res_send, res_all, ss_all, normed, q_send, q_all, qa, qc, att_send, att_all, att_x,
    gu_send, gu_all, hid, rs_send, rs_all, head_out,
    qkv_sem, out_sem, gate_sem, up_sem, down_sem, kv_sem,
    res_s, res_r, ss_s, ss_r, q_s, q_r, att_s, att_r, gu_s, gu_r, hid_s, hid_r, rs_s, rs_r,
):
    nx, ny = sizes["gx"], sizes["gy"]
    n = nx * ny
    g, i, j = lax.axis_index("groups"), lax.axis_index("gx"), lax.axis_index("gy")
    me = i * ny + j
    rows = res_ref.shape[0]
    own_rows = q_send.shape[1]
    half = res_ref.shape[1] // 2
    chunks, _, cols = gate_w.shape
    part = cols // ny
    ychunks, _, ycols = down_w.shape
    heads = qa.shape[1] - 8
    f32, bf16 = jnp.float32, jnp.bfloat16

    def peer(d):
        other = lax.rem(me + d, n)
        return (g, other // ny, lax.rem(other, ny)), other

    def gate_copy(c):
        return pltpu.make_async_copy(
            gate_hbm.at[:, pl.ds(pl.multiple_of(c * cols, cols), cols)], gate_w.at[c], gate_sem.at[c])

    def up_copy(c):
        return pltpu.make_async_copy(
            up_hbm.at[:, pl.ds(pl.multiple_of(c * cols, cols), cols)], up_w.at[c], up_sem.at[c])

    def down_copy(c):
        return pltpu.make_async_copy(
            down_hbm.at[:, pl.ds(pl.multiple_of(c * ycols, ycols), ycols)], down_w.at[c], down_sem.at[c])

    qkv_copy = pltpu.make_async_copy(qkv_hbm, qkv_w, qkv_sem)
    out_copy = pltpu.make_async_copy(out_hbm, out_w, out_sem)
    keys_copy = pltpu.make_async_copy(keys_hbm, keys_v, kv_sem.at[0])
    vals_copy = pltpu.make_async_copy(vals_hbm, vals_v, kv_sem.at[1])

    qkv_copy.start()
    keys_copy.start()
    vals_copy.start()

    def start_gu(c, carry):
        gate_copy(c).start()
        up_copy(c).start()
        return carry

    lax.fori_loop(0, chunks, start_gu, 0)
    out_copy.start()

    def start_down(c, carry):
        down_copy(c).start()
        return carry

    lax.fori_loop(0, ychunks, start_down, 0)

    barrier = pltpu.get_barrier_semaphore()

    def greet(d, carry):
        target, _ = peer(d)
        pl.semaphore_signal(barrier, inc=1, device_id=target, device_id_type=MESH)
        return carry

    lax.fori_loop(1, n, greet, 0)

    own = res_ref[...].astype(f32)
    packed = jnp.concatenate([own[:, :half], own[:, half:]], axis=0).astype(bf16)
    res_send[...] = packed
    res_all[i] = packed
    squares = jnp.sum(own * own, axis=1, keepdims=True)
    diagonal = lax.broadcasted_iota(jnp.int32, (rows, LANES), 0) == lax.broadcasted_iota(
        jnp.int32, (rows, LANES), 1)
    in_lanes = jnp.sum(jnp.where(diagonal, squares, 0.0), axis=0, keepdims=True)
    ss_all[me] = in_lanes

    pl.semaphore_wait(barrier, n - 1)

    def send_res(d, carry):
        to = lax.rem(i + d, nx)
        pltpu.make_async_remote_copy(
            src_ref=res_send, dst_ref=res_all.at[i], send_sem=res_s, recv_sem=res_r,
            device_id=(g, to, j), device_id_type=MESH).start()
        return carry

    def send_ss(d, carry):
        target, _ = peer(d)
        pltpu.make_async_remote_copy(
            src_ref=ss_all.at[me], dst_ref=ss_all.at[me], send_sem=ss_s, recv_sem=ss_r,
            device_id=target, device_id_type=MESH).start()
        return carry

    lax.fori_loop(1, nx, send_res, 0)
    lax.fori_loop(1, n, send_ss, 0)

    def drain(ref, sem):
        pltpu.make_async_copy(ref, ref, sem).wait()

    drain(ss_all.at[pl.ds(0, n - 1)], ss_r)
    drain(res_all.at[pl.ds(0, nx - 1)], res_r)

    gain = gain_ref[...].astype(f32)
    blocks = []
    for block in range(nx):
        lanes = ss_all[block * ny]
        for other in range(1, ny):
            lanes = lanes + ss_all[block * ny + other]
        total = jnp.sum(jnp.where(diagonal, lanes, 0.0), axis=1, keepdims=True)
        scale = lax.rsqrt(total / D + 1e-06)
        wide = res_all[block].astype(f32)
        wide = jnp.concatenate([wide[:rows], wide[rows:]], axis=1)
        blocks.append(wide * scale * gain)
    normed[...] = jnp.concatenate(blocks, axis=0).astype(bf16)

    qkv_copy.wait()
    qkv_part = jnp.dot(normed[...], qkv_w[...], preferred_element_type=f32)
    for to in range(n):
        q_send[to] = qkv_part[to * own_rows:(to + 1) * own_rows, :]
    q_all[me] = q_send[me]

    def send_q(d, carry):
        target, other = peer(d)
        pltpu.make_async_remote_copy(
            src_ref=q_send.at[other], dst_ref=q_all.at[me], send_sem=q_s, recv_sem=q_r,
            device_id=target, device_id_type=MESH).start()
        return carry

    lax.fori_loop(1, n, send_q, 0)

    def gu_step(c, carry):
        gate_copy(c).wait()
        gate = jnp.dot(normed[...], gate_w[c], preferred_element_type=f32).astype(bf16)
        for to in range(ny):
            gu_send[c, to, 0] = gate[:, to * part:(to + 1) * part]
        up_copy(c).wait()
        up = jnp.dot(normed[...], up_w[c], preferred_element_type=f32).astype(bf16)
        for to in range(ny):
            gu_send[c, to, 1] = up[:, to * part:(to + 1) * part]
        gu_all[c, j] = gu_send[c, j]

        def send_gu(d, inner):
            to = lax.rem(j + d, ny)
            pltpu.make_async_remote_copy(
                src_ref=gu_send.at[c, to], dst_ref=gu_all.at[c, j], send_sem=gu_s,
                recv_sem=gu_r.at[c], device_id=(g, i, to), device_id_type=MESH).start()
            return inner

        lax.fori_loop(1, ny, send_gu, 0)
        return carry

    def hid_step(c, carry):
        drain(gu_all.at[c, pl.ds(0, ny - 1)], gu_r.at[c])
        gate = gu_all[c, 0, 0].astype(f32)
        up = gu_all[c, 0, 1].astype(f32)
        for other in range(1, ny):
            gate = gate + gu_all[c, other, 0].astype(f32)
            up = up + gu_all[c, other, 1].astype(f32)
        here = hid.at[:, pl.ds(pl.multiple_of(c * cols + j * part, part), part)]
        here[...] = (gate / (1.0 + jnp.exp(-gate)) * up).astype(bf16)

        def send_hid(d, inner):
            to = lax.rem(j + d, ny)
            pltpu.make_async_remote_copy(
                src_ref=here, dst_ref=here, send_sem=hid_s, recv_sem=hid_r,
                device_id=(g, i, to), device_id_type=MESH).start()
            return inner

        lax.fori_loop(1, ny, send_hid, 0)
        return carry

    early = sizes["early"]
    lag = sizes["lag"]
    lax.fori_loop(0, early, gu_step, 0)

    drain(q_all.at[pl.ds(0, n - 1)], q_r)
    per = q_all.shape[2] // LANES
    for block in range(nx):
        summed = q_all[block * ny]
        for other in range(1, ny):
            summed = summed + q_all[block * ny + other]
        summed = summed.astype(bf16).astype(f32)
        for at in range(per):
            index = block * per + at
            into = qa if index % 2 == 0 else qc
            for r in range(own_rows):
                into[r, index // 2:index // 2 + 1, :] = summed[r:r + 1, at * LANES:(at + 1) * LANES]
    keys_copy.wait()
    vals_copy.wait()
    context = keys_v.shape[1]
    score_scale = keys_v.shape[2] ** (-0.5)
    per_block = heads // nx
    for r in range(own_rows):
        turn = freq_ref[...] * pos_ref[r].astype(f32)
        cosine, sine = jnp.cos(turn), jnp.sin(turn)

        def rotated(a, c):
            return jnp.concatenate([a * cosine - c * sine, a * sine + c * cosine], axis=1).astype(bf16)

        queries = rotated(qa[r, 0:heads, :], qc[r, 0:heads, :])
        new_key = rotated(qa[r, heads:heads + 1, :], qc[r, heads:heads + 1, :])
        new_value = jnp.concatenate(
            [qa[r, heads + 1:heads + 2, :], qc[r, heads + 1:heads + 2, :]], axis=1)
        scores = lax.dot_general(
            queries, keys_v[r], (((1,), (1,)), ((), ())), preferred_element_type=f32) * score_scale
        visible = lax.broadcasted_iota(jnp.int32, (heads, context), 1) < len_ref[r]
        scores = jnp.where(visible, scores, -jnp.inf)
        own_score = jnp.sum(
            queries.astype(f32) * new_key.astype(f32), axis=1, keepdims=True) * score_scale
        top = jnp.maximum(jnp.max(scores, axis=1, keepdims=True), own_score)
        shifted = jnp.exp(scores - top)
        own_shifted = jnp.exp(own_score - top)
        total = jnp.sum(shifted, axis=1, keepdims=True) + own_shifted
        weights = (shifted / total).astype(bf16)
        own_weight = (own_shifted / total).astype(bf16).astype(f32)
        mixed = jnp.dot(weights, vals_v[r], preferred_element_type=f32) + own_weight * new_value
        mixed = mixed.astype(bf16).astype(f32)
        width = mixed.shape[1]
        for h in range(heads):
            at = h % per_block
            att_send[h // per_block, r:r + 1, at * width:(at + 1) * width] = mixed[h:h + 1, :]
    att_all[me] = att_send[i]

    def send_att(d, carry):
        target, other = peer(d)
        pltpu.make_async_remote_copy(
            src_ref=att_send.at[other // ny], dst_ref=att_all.at[me], send_sem=att_s,
            recv_sem=att_r, device_id=target, device_id_type=MESH).start()
        return carry

    lax.fori_loop(1, n, send_att, 0)

    def both(c, carry):
        gu_step(c, 0)
        hid_step(c - lag, 0)
        return carry

    lax.fori_loop(early, lag, gu_step, 0)
    lax.fori_loop(max(early, lag), chunks, both, 0)
    lax.fori_loop(max(chunks - lag, 0), chunks, hid_step, 0)

    drain(att_all.at[pl.ds(0, n - 1)], att_r)
    for source in range(n):
        att_x[source * own_rows:(source + 1) * own_rows, :] = att_all[source]
    out_copy.wait()
    attended = att_x[...].astype(bf16)

    def out_step(c, carry):
        at = pl.ds(pl.multiple_of(c * ycols, ycols), ycols)
        head_out[c] = jnp.dot(attended, out_w[:, at], preferred_element_type=f32)
        return carry

    lax.fori_loop(0, ychunks, out_step, 0)

    drain(hid.at[:, pl.ds(0, chunks * part * (ny - 1))], hid_r)

    def down_step(c, carry):
        down_copy(c).wait()
        term = head_out[c] + jnp.dot(hid[...], down_w[c], preferred_element_type=f32)
        for to in range(nx):
            mine = term[to * rows:(to + 1) * rows]
            rs_send[c, to] = jnp.concatenate(
                [mine[:, :ycols // 2], mine[:, ycols // 2:]], axis=0).astype(bf16)
        rs_all[c, i] = rs_send[c, i]

        def send_rs(d, inner):
            to = lax.rem(i + d, nx)
            pltpu.make_async_remote_copy(
                src_ref=rs_send.at[c, to], dst_ref=rs_all.at[c, i], send_sem=rs_s,
                recv_sem=rs_r.at[c], device_id=(g, to, j), device_id_type=MESH).start()
            return inner

        lax.fori_loop(1, nx, send_rs, 0)
        return carry

    lax.fori_loop(0, ychunks, down_step, 0)

    for c in range(ychunks):
        drain(rs_all.at[c, pl.ds(0, nx - 1)], rs_r.at[c])
        total = rs_all[c, 0].astype(f32)
        for other in range(1, nx):
            total = total + rs_all[c, other].astype(f32)
        y_ref[:, c * ycols:(c + 1) * ycols] = jnp.concatenate(
            [total[:rows], total[rows:]], axis=1).astype(bf16)

    def drain_res(d, carry):
        drain(res_send, res_s)
        return carry

    lax.fori_loop(1, nx, drain_res, 0)
    drain(ss_all.at[pl.ds(0, n - 1)], ss_s)
    drain(q_all.at[pl.ds(0, n - 1)], q_s)
    drain(att_all.at[pl.ds(0, n - 1)], att_s)
    drain(gu_all.at[:, pl.ds(0, ny - 1)], gu_s)
    drain(hid.at[:, pl.ds(0, chunks * part * (ny - 1))], hid_s)
    drain(rs_all.at[:, pl.ds(0, nx - 1)], rs_s)


def kernel_shards(
    nx,
    ny,
    residual,
    norm_gain,
    qkv_weight,
    out_weight,
    gate_weight,
    up_weight,
    down_weight,
    cache_keys,
    cache_values,
    lengths,
    positions,
):
    n = nx * ny
    rows, features = residual.shape
    own_rows, context, width = cache_keys.shape
    batch = rows * nx
    qkv_cols = qkv_weight.shape[1]
    heads = out_weight.shape[0] * nx // width
    units = gate_weight.shape[1]
    cols = LANES * ny
    chunks = units // cols
    ycols = 512
    ychunks = features // ycols
    half = width // 2
    frequency = np.exp(np.arange(half) * (-2.0 * np.log(10000.0) / width)).astype(np.float32)
    f32, bf16 = jnp.float32, jnp.bfloat16
    sem = pltpu.SemaphoreType.DMA
    vmem = pl.BlockSpec(memory_space=pltpu.VMEM)
    smem = pl.BlockSpec(memory_space=pltpu.SMEM)
    hbm = pl.BlockSpec(memory_space=pl.ANY)
    sizes = {"gx": nx, "gy": ny, "early": 2, "lag": 4}
    return pl.pallas_call(
        functools.partial(block_kernel, sizes),
        out_shape=jax.ShapeDtypeStruct((rows, features), bf16),
        in_specs=[vmem, vmem, vmem] + [hbm] * 7 + [smem, smem],
        out_specs=vmem,
        scratch_shapes=[
            pltpu.VMEM((features, qkv_cols), bf16),
            pltpu.VMEM(out_weight.shape, bf16),
            pltpu.VMEM((chunks, features, cols), bf16),
            pltpu.VMEM((chunks, features, cols), bf16),
            pltpu.VMEM((ychunks, units, ycols), bf16),
            pltpu.VMEM(cache_keys.shape, bf16),
            pltpu.VMEM(cache_values.shape, bf16),
            pltpu.VMEM((2 * rows, features // 2), bf16),
            pltpu.VMEM((nx, 2 * rows, features // 2), bf16),
            pltpu.VMEM((n, 1, LANES), f32),
            pltpu.VMEM((batch, features), bf16),
            pltpu.VMEM((n, own_rows, qkv_cols), f32),
            pltpu.VMEM((n, own_rows, qkv_cols), f32),
            pltpu.VMEM((own_rows, heads + 8, half), f32),
            pltpu.VMEM((own_rows, heads + 8, half), f32),
            pltpu.VMEM((nx, own_rows, heads // nx * width), f32),
            pltpu.VMEM((n, own_rows, heads // nx * width), f32),
            pltpu.VMEM((batch, heads // nx * width), f32),
            pltpu.VMEM((chunks, ny, 2, batch, LANES), bf16),
            pltpu.VMEM((chunks, ny, 2, batch, LANES), bf16),
            pltpu.VMEM((batch, units), bf16),
            pltpu.VMEM((ychunks, nx, 2 * rows, ycols // 2), bf16),
            pltpu.VMEM((ychunks, nx, 2 * rows, ycols // 2), bf16),
            pltpu.VMEM((ychunks, batch, ycols), f32),
            sem, sem, sem((chunks,)), sem((chunks,)), sem((ychunks,)), sem((2,)),
            sem, sem, sem, sem, sem, sem, sem, sem,
            sem, sem((chunks,)), sem, sem, sem, sem((ychunks,)),
        ],
        compiler_params=pltpu.CompilerParams(
            collective_id=0, has_side_effects=True, vmem_limit_bytes=64 * 1024 * 1024 - 65536),
    )(
        residual,
        norm_gain.reshape(1, features),
        jnp.asarray(frequency).reshape(1, half),
        qkv_weight,
        out_weight,
        gate_weight,
        up_weight,
        down_weight,
        cache_keys,
        cache_values,
        lengths,
        positions,
    )


def fits_kernel(nx, ny, residual, qkv_weight, out_weight, gate_weight, cache_keys):
    rows, features = residual.shape
    own_rows, _, width = cache_keys.shape
    units = gate_weight.shape[1]
    held = features * (qkv_weight.shape[1] + 3 * units) + out_weight.size + 2 * cache_keys.size
    return (
        rows == 8
        and rows == own_rows * ny
        and width == 2 * LANES
        and qkv_weight.shape[1] % LANES == 0
        and out_weight.shape[0] % width == 0
        and units % (LANES * ny) == 0
        and units // (LANES * ny) >= 4
        and features % 512 == 0
        and 2 * held <= 58 * 1024 * 1024
    )


def shards(nx, ny, *operands):
    residual, _, qkv_weight, out_weight, gate_weight, _, _, cache_keys = operands[:8]
    if fits_kernel(nx, ny, residual, qkv_weight, out_weight, gate_weight, cache_keys):
        return kernel_shards(nx, ny, *operands)
    return collective_shards(*operands)


def solution(mesh):
    in_specs = (
        P(("groups", "gx"), "gy"),
        P("gy"),
        P("gy", "gx"),
        P("gx", "gy"),
        P("gy", "gx"),
        P("gy", "gx"),
        P("gx", "gy"),
        P(("groups", "gx", "gy"), None, None),
        P(("groups", "gx", "gy"), None, None),
        P(("groups", "gx", "gy")),
        P(("groups", "gx", "gy")),
    )
    out_specs = P(("groups", "gx"), "gy")
    body = functools.partial(shards, mesh.shape["gx"], mesh.shape["gy"])
    return jax.shard_map(body, mesh=mesh, in_specs=in_specs, out_specs=out_specs, check_vma=False)
```

```python
import functools

import jax
import jax.numpy as jnp
import numpy as np
from jax import lax
from jax.experimental import pallas as pl
from jax.experimental.pallas import tpu as pltpu
from jax.sharding import PartitionSpec as P

D = 8192
LANES = 128
MESH = pl.DeviceIdType.MESH


def angles(token_positions, head_width):
    half_width = head_width // 2
    frequency = jnp.exp(
        jnp.arange(half_width, dtype=jnp.float32) * (-2.0 * jnp.log(10000.0) / head_width)
    )
    return token_positions.astype(jnp.float32)[:, None] * frequency[None, :]


def rotary(vectors, turn):
    half_width = vectors.shape[-1] // 2
    first_half = vectors[..., :half_width]
    second_half = vectors[..., half_width:]
    cosine = jnp.cos(turn)
    sine_part = jnp.sin(turn)
    return jnp.concatenate(
        [
            first_half * cosine - second_half * sine_part,
            first_half * sine_part + second_half * cosine,
        ],
        axis=-1,
    )


def attend(joined, cached_keys, cached_values, valid_lengths, token_positions):
    row_count = joined.shape[0]
    head_width = cached_keys.shape[2]
    query_width = joined.shape[1] - 2 * head_width
    head_count = query_width // head_width
    queries = joined[:, :query_width].astype(jnp.float32).reshape(row_count, head_count, head_width)
    new_key = joined[:, query_width : query_width + head_width].astype(jnp.float32)
    new_value = joined[:, query_width + head_width :].astype(jnp.float32)
    turn = angles(token_positions, head_width)
    rotated_queries = rotary(queries, turn[:, None, :]).astype(jnp.bfloat16)
    rotated_key = rotary(new_key, turn).astype(jnp.bfloat16)
    score_scale = head_width ** (-0.5)
    scores = (
        jnp.einsum("rhd,rcd->rhc", rotated_queries, cached_keys, preferred_element_type=jnp.float32)
        * score_scale
    )
    visible = (
        jnp.arange(cached_keys.shape[1], dtype=jnp.int32)[None, None, :]
        < valid_lengths[:, None, None]
    )
    scores = jnp.where(visible, scores, -jnp.inf)
    own_score = (
        jnp.einsum("rhd,rd->rh", rotated_queries, rotated_key, preferred_element_type=jnp.float32)
        * score_scale
    )
    top_score = jnp.maximum(jnp.max(scores, axis=2), own_score)
    shifted = jnp.exp(scores - top_score[:, :, None])
    own_shifted = jnp.exp(own_score - top_score)
    denominator = jnp.sum(shifted, axis=2) + own_shifted
    softmax_weights = (shifted / denominator[:, :, None]).astype(jnp.bfloat16)
    own_weight = (own_shifted / denominator).astype(jnp.bfloat16)
    mixed = jnp.einsum(
        "rhc,rcd->rhd", softmax_weights, cached_values, preferred_element_type=jnp.float32
    )
    mixed = mixed + own_weight.astype(jnp.float32)[:, :, None] * new_value[:, None, :]
    return mixed.reshape(row_count, query_width).astype(jnp.bfloat16)


def collective_shards(
    residual,
    norm_gain,
    qkv_weight,
    out_weight,
    gate_weight,
    up_weight,
    down_weight,
    cache_keys,
    cache_values,
    lengths,
    positions,
):
    gain_wide = norm_gain.astype(jnp.float32)
    widened = residual.astype(jnp.float32)
    totals = lax.psum(jnp.sum(widened * widened, axis=1), "gy")
    scaled_rows = (widened * lax.rsqrt(totals / D + 1e-06)[:, None] * gain_wide).astype(
        jnp.bfloat16
    )
    normed = lax.all_gather(scaled_rows, "gx", axis=0, tiled=True)
    qkv_part = jnp.dot(normed, qkv_weight, preferred_element_type=jnp.float32)
    gate_part = jnp.dot(normed, gate_weight, preferred_element_type=jnp.float32)
    up_part = jnp.dot(normed, up_weight, preferred_element_type=jnp.float32)
    swapped = lax.all_to_all(qkv_part, "gx", split_axis=0, concat_axis=1, tiled=True)
    rows_qkv = lax.psum_scatter(swapped, "gy", scatter_dimension=0, tiled=True).astype(jnp.bfloat16)
    attended = attend(rows_qkv, cache_keys, cache_values, lengths, positions)
    grouped = lax.all_gather(attended, "gy", axis=0, tiled=True)
    heads_out = lax.all_to_all(grouped, "gx", split_axis=1, concat_axis=0, tiled=True)
    gate_sum, up_sum = lax.psum((gate_part, up_part), "gy")
    hidden = (jax.nn.silu(gate_sum) * up_sum).astype(jnp.bfloat16)
    block_term = jnp.dot(heads_out, out_weight, preferred_element_type=jnp.float32)
    return lax.psum_scatter(
        (block_term + jnp.dot(hidden, down_weight, preferred_element_type=jnp.float32)).astype(
            jnp.bfloat16
        ),
        "gx",
        scatter_dimension=0,
        tiled=True,
    )


def block_kernel(
    sizes,
    res_ref, gain_ref, freq_ref, qkv_hbm, out_hbm, gate_hbm, up_hbm, down_hbm, keys_hbm, vals_hbm,
    len_ref, pos_ref,
    y_ref,
    qkv_w, out_w, gate_w, up_w, down_w, keys_v, vals_v,
    res_send, res_all, ss_all, normed, q_send, q_all, qa, qc, att_send, att_all, att_x,
    gu_send, gu_all, hid, rs_send, rs_all, head_out,
    qkv_sem, out_sem, gate_sem, up_sem, down_sem, kv_sem,
    res_s, res_r, ss_s, ss_r, q_s, q_r, att_s, att_r, gu_s, gu_r, hid_s, hid_r, rs_s, rs_r,
):
    nx, ny = sizes["gx"], sizes["gy"]
    n = nx * ny
    g, i, j = lax.axis_index("groups"), lax.axis_index("gx"), lax.axis_index("gy")
    me = i * ny + j
    rows = res_ref.shape[0]
    own_rows = q_send.shape[1]
    half = res_ref.shape[1] // 2
    chunks, _, cols = gate_w.shape
    part = cols // ny
    ychunks, _, ycols = down_w.shape
    heads = qa.shape[1] - 8
    f32, bf16 = jnp.float32, jnp.bfloat16

    def peer(d):
        other = lax.rem(me + d, n)
        return (g, other // ny, lax.rem(other, ny)), other

    def gate_copy(c):
        return pltpu.make_async_copy(
            gate_hbm.at[:, pl.ds(pl.multiple_of(c * cols, cols), cols)], gate_w.at[c], gate_sem.at[c])

    def up_copy(c):
        return pltpu.make_async_copy(
            up_hbm.at[:, pl.ds(pl.multiple_of(c * cols, cols), cols)], up_w.at[c], up_sem.at[c])

    def down_copy(c):
        return pltpu.make_async_copy(
            down_hbm.at[:, pl.ds(pl.multiple_of(c * ycols, ycols), ycols)], down_w.at[c], down_sem.at[c])

    qkv_copy = pltpu.make_async_copy(qkv_hbm, qkv_w, qkv_sem)
    out_copy = pltpu.make_async_copy(out_hbm, out_w, out_sem)
    keys_copy = pltpu.make_async_copy(keys_hbm, keys_v, kv_sem.at[0])
    vals_copy = pltpu.make_async_copy(vals_hbm, vals_v, kv_sem.at[1])

    qkv_copy.start()
    keys_copy.start()
    vals_copy.start()

    def start_gu(c, carry):
        gate_copy(c).start()
        up_copy(c).start()
        return carry

    lax.fori_loop(0, chunks, start_gu, 0)
    out_copy.start()

    def start_down(c, carry):
        down_copy(c).start()
        return carry

    lax.fori_loop(0, ychunks, start_down, 0)

    barrier = pltpu.get_barrier_semaphore()

    def greet(d, carry):
        target, _ = peer(d)
        pl.semaphore_signal(barrier, inc=1, device_id=target, device_id_type=MESH)
        return carry

    lax.fori_loop(1, n, greet, 0)

    own = res_ref[...].astype(f32)
    packed = jnp.concatenate([own[:, :half], own[:, half:]], axis=0).astype(bf16)
    res_send[...] = packed
    res_all[i] = packed
    squares = jnp.sum(own * own, axis=1, keepdims=True)
    diagonal = lax.broadcasted_iota(jnp.int32, (rows, LANES), 0) == lax.broadcasted_iota(
        jnp.int32, (rows, LANES), 1)
    in_lanes = jnp.sum(jnp.where(diagonal, squares, 0.0), axis=0, keepdims=True)
    ss_all[me] = in_lanes

    pl.semaphore_wait(barrier, n - 1)

    def send_res(d, carry):
        to = lax.rem(i + d, nx)
        pltpu.make_async_remote_copy(
            src_ref=res_send, dst_ref=res_all.at[i], send_sem=res_s, recv_sem=res_r,
            device_id=(g, to, j), device_id_type=MESH).start()
        return carry

    def send_ss(d, carry):
        target, _ = peer(d)
        pltpu.make_async_remote_copy(
            src_ref=ss_all.at[me], dst_ref=ss_all.at[me], send_sem=ss_s, recv_sem=ss_r,
            device_id=target, device_id_type=MESH).start()
        return carry

    lax.fori_loop(1, nx, send_res, 0)
    lax.fori_loop(1, n, send_ss, 0)

    def drain(ref, sem):
        pltpu.make_async_copy(ref, ref, sem).wait()

    drain(ss_all.at[pl.ds(0, n - 1)], ss_r)
    drain(res_all.at[pl.ds(0, nx - 1)], res_r)

    gain = gain_ref[...].astype(f32).reshape(1, 2 * half)
    blocks = []
    for block in range(nx):
        lanes = ss_all[block * ny]
        for other in range(1, ny):
            lanes = lanes + ss_all[block * ny + other]
        total = jnp.sum(jnp.where(diagonal, lanes, 0.0), axis=1, keepdims=True)
        scale = lax.rsqrt(total / D + 1e-06)
        wide = res_all[block].astype(f32)
        wide = jnp.concatenate([wide[:rows], wide[rows:]], axis=1)
        blocks.append(wide * scale * gain)
    normed[...] = jnp.concatenate(blocks, axis=0).astype(bf16)

    qkv_copy.wait()
    qkv_part = jnp.dot(normed[...], qkv_w[...], preferred_element_type=f32)
    for to in range(n):
        q_send[to] = qkv_part[to * own_rows:(to + 1) * own_rows, :]
    q_all[me] = q_send[me]

    def send_q(d, carry):
        target, other = peer(d)
        pltpu.make_async_remote_copy(
            src_ref=q_send.at[other], dst_ref=q_all.at[me], send_sem=q_s, recv_sem=q_r,
            device_id=target, device_id_type=MESH).start()
        return carry

    lax.fori_loop(1, n, send_q, 0)

    def gu_step(c, carry):
        gate_copy(c).wait()
        gate = jnp.dot(normed[...], gate_w[c], preferred_element_type=f32).astype(bf16)
        for to in range(ny):
            gu_send[c, to, 0] = gate[:, to * part:(to + 1) * part]
        up_copy(c).wait()
        up = jnp.dot(normed[...], up_w[c], preferred_element_type=f32).astype(bf16)
        for to in range(ny):
            gu_send[c, to, 1] = up[:, to * part:(to + 1) * part]
        gu_all[c, j] = gu_send[c, j]

        def send_gu(d, inner):
            to = lax.rem(j + d, ny)
            pltpu.make_async_remote_copy(
                src_ref=gu_send.at[c, to], dst_ref=gu_all.at[c, j], send_sem=gu_s,
                recv_sem=gu_r.at[c], device_id=(g, i, to), device_id_type=MESH).start()
            return inner

        lax.fori_loop(1, ny, send_gu, 0)
        return carry

    def hid_step(c, carry):
        drain(gu_all.at[c, pl.ds(0, ny - 1)], gu_r.at[c])
        gate = gu_all[c, 0, 0].astype(f32)
        up = gu_all[c, 0, 1].astype(f32)
        for other in range(1, ny):
            gate = gate + gu_all[c, other, 0].astype(f32)
            up = up + gu_all[c, other, 1].astype(f32)
        here = hid.at[:, pl.ds(pl.multiple_of(c * cols + j * part, part), part)]
        here[...] = (gate / (1.0 + jnp.exp(-gate)) * up).astype(bf16)

        def send_hid(d, inner):
            to = lax.rem(j + d, ny)
            pltpu.make_async_remote_copy(
                src_ref=here, dst_ref=here, send_sem=hid_s, recv_sem=hid_r,
                device_id=(g, i, to), device_id_type=MESH).start()
            return inner

        lax.fori_loop(1, ny, send_hid, 0)
        return carry

    early = sizes["early"]
    lag = sizes["lag"]

    def both(c, carry):
        gu_step(c, 0)
        hid_step(c - lag, 0)
        return carry

    def run(first, end):
        middle = min(max(first, lag), end)
        lax.fori_loop(first, middle, gu_step, 0)
        lax.fori_loop(middle, end, both, 0)

    run(0, early)

    drain(q_all.at[pl.ds(0, n - 1)], q_r)
    per = q_all.shape[2] // LANES
    for block in range(nx):
        summed = q_all[block * ny]
        for other in range(1, ny):
            summed = summed + q_all[block * ny + other]
        summed = summed.astype(bf16).astype(f32)
        for at in range(per):
            index = block * per + at
            into = qa if index % 2 == 0 else qc
            for r in range(own_rows):
                into[r, index // 2:index // 2 + 1, :] = summed[r:r + 1, at * LANES:(at + 1) * LANES]
    keys_copy.wait()
    vals_copy.wait()
    context = keys_v.shape[1]
    score_scale = keys_v.shape[2] ** (-0.5)
    per_block = heads // nx
    for r in range(own_rows):
        turn = freq_ref[...] * pos_ref[r].astype(f32)
        cosine, sine = jnp.cos(turn), jnp.sin(turn)

        def rotated(a, c):
            return jnp.concatenate([a * cosine - c * sine, a * sine + c * cosine], axis=1).astype(bf16)

        queries = rotated(qa[r, 0:heads, :], qc[r, 0:heads, :])
        new_key = rotated(qa[r, heads:heads + 1, :], qc[r, heads:heads + 1, :])
        new_value = jnp.concatenate(
            [qa[r, heads + 1:heads + 2, :], qc[r, heads + 1:heads + 2, :]], axis=1)
        scores = lax.dot_general(
            queries, keys_v[r], (((1,), (1,)), ((), ())), preferred_element_type=f32) * score_scale
        visible = lax.broadcasted_iota(jnp.int32, (heads, context), 1) < len_ref[r]
        scores = jnp.where(visible, scores, -jnp.inf)
        own_score = jnp.sum(
            queries.astype(f32) * new_key.astype(f32), axis=1, keepdims=True) * score_scale
        top = jnp.maximum(jnp.max(scores, axis=1, keepdims=True), own_score)
        shifted = jnp.exp(scores - top)
        own_shifted = jnp.exp(own_score - top)
        total = jnp.sum(shifted, axis=1, keepdims=True) + own_shifted
        weights = (shifted / total).astype(bf16)
        own_weight = (own_shifted / total).astype(bf16).astype(f32)
        mixed = jnp.dot(weights, vals_v[r], preferred_element_type=f32) + own_weight * new_value
        mixed = mixed.astype(bf16).astype(f32)
        width = mixed.shape[1]
        for h in range(heads):
            at = h % per_block
            att_send[h // per_block, r:r + 1, at * width:(at + 1) * width] = mixed[h:h + 1, :]
    att_all[me] = att_send[i]

    def send_att(d, carry):
        target, other = peer(d)
        pltpu.make_async_remote_copy(
            src_ref=att_send.at[other // ny], dst_ref=att_all.at[me], send_sem=att_s,
            recv_sem=att_r, device_id=target, device_id_type=MESH).start()
        return carry

    lax.fori_loop(1, n, send_att, 0)

    run(early, chunks)
    lax.fori_loop(chunks - lag, chunks, hid_step, 0)

    drain(att_all.at[pl.ds(0, n - 1)], att_r)
    for source in range(n):
        att_x[source * own_rows:(source + 1) * own_rows, :] = att_all[source]
    out_copy.wait()
    attended = att_x[...].astype(bf16)

    def out_step(c, carry):
        at = pl.ds(pl.multiple_of(c * ycols, ycols), ycols)
        head_out[c] = jnp.dot(attended, out_w[:, at], preferred_element_type=f32)
        return carry

    lax.fori_loop(0, ychunks, out_step, 0)

    drain(hid.at[:, pl.ds(0, chunks * part * (ny - 1))], hid_r)

    def down_step(c, carry):
        down_copy(c).wait()
        term = head_out[c] + jnp.dot(hid[...], down_w[c], preferred_element_type=f32)
        for to in range(nx):
            mine = term[to * rows:(to + 1) * rows]
            rs_send[c, to] = jnp.concatenate(
                [mine[:, :ycols // 2], mine[:, ycols // 2:]], axis=0).astype(bf16)
        rs_all[c, i] = rs_send[c, i]

        def send_rs(d, inner):
            to = lax.rem(i + d, nx)
            pltpu.make_async_remote_copy(
                src_ref=rs_send.at[c, to], dst_ref=rs_all.at[c, i], send_sem=rs_s,
                recv_sem=rs_r.at[c], device_id=(g, to, j), device_id_type=MESH).start()
            return inner

        lax.fori_loop(1, nx, send_rs, 0)
        return carry

    lax.fori_loop(0, ychunks, down_step, 0)

    for c in range(ychunks):
        drain(rs_all.at[c, pl.ds(0, nx - 1)], rs_r.at[c])
        total = rs_all[c, 0].astype(f32)
        for other in range(1, nx):
            total = total + rs_all[c, other].astype(f32)
        y_ref[:, c * ycols:(c + 1) * ycols] = jnp.concatenate(
            [total[:rows], total[rows:]], axis=1).astype(bf16)

    def drain_res(d, carry):
        drain(res_send, res_s)
        return carry

    lax.fori_loop(1, nx, drain_res, 0)
    drain(ss_all.at[pl.ds(0, n - 1)], ss_s)
    drain(q_all.at[pl.ds(0, n - 1)], q_s)
    drain(att_all.at[pl.ds(0, n - 1)], att_s)
    drain(gu_all.at[:, pl.ds(0, ny - 1)], gu_s)
    drain(hid.at[:, pl.ds(0, chunks * part * (ny - 1))], hid_s)
    drain(rs_all.at[:, pl.ds(0, nx - 1)], rs_s)


def kernel_shards(
    nx,
    ny,
    residual,
    norm_gain,
    qkv_weight,
    out_weight,
    gate_weight,
    up_weight,
    down_weight,
    cache_keys,
    cache_values,
    lengths,
    positions,
):
    n = nx * ny
    rows, features = residual.shape
    own_rows, context, width = cache_keys.shape
    batch = rows * nx
    qkv_cols = qkv_weight.shape[1]
    heads = out_weight.shape[0] * nx // width
    units = gate_weight.shape[1]
    cols = LANES * ny
    chunks = units // cols
    ycols = 512
    ychunks = features // ycols
    half = width // 2
    frequency = np.exp(np.arange(half) * (-2.0 * np.log(10000.0) / width)).astype(np.float32)
    f32, bf16 = jnp.float32, jnp.bfloat16
    sem = pltpu.SemaphoreType.DMA
    vmem = pl.BlockSpec(memory_space=pltpu.VMEM)
    smem = pl.BlockSpec(memory_space=pltpu.SMEM)
    hbm = pl.BlockSpec(memory_space=pl.ANY)
    sizes = {"gx": nx, "gy": ny, "early": min(7, chunks), "lag": min(6, chunks)}
    return pl.pallas_call(
        functools.partial(block_kernel, sizes),
        out_shape=jax.ShapeDtypeStruct((rows, features), bf16),
        in_specs=[vmem, vmem, vmem] + [hbm] * 7 + [smem, smem],
        out_specs=vmem,
        scratch_shapes=[
            pltpu.VMEM((features, qkv_cols), bf16),
            pltpu.VMEM(out_weight.shape, bf16),
            pltpu.VMEM((chunks, features, cols), bf16),
            pltpu.VMEM((chunks, features, cols), bf16),
            pltpu.VMEM((ychunks, units, ycols), bf16),
            pltpu.VMEM(cache_keys.shape, bf16),
            pltpu.VMEM(cache_values.shape, bf16),
            pltpu.VMEM((2 * rows, features // 2), bf16),
            pltpu.VMEM((nx, 2 * rows, features // 2), bf16),
            pltpu.VMEM((n, 1, LANES), f32),
            pltpu.VMEM((batch, features), bf16),
            pltpu.VMEM((n, own_rows, qkv_cols), f32),
            pltpu.VMEM((n, own_rows, qkv_cols), f32),
            pltpu.VMEM((own_rows, heads + 8, half), f32),
            pltpu.VMEM((own_rows, heads + 8, half), f32),
            pltpu.VMEM((nx, own_rows, heads // nx * width), f32),
            pltpu.VMEM((n, own_rows, heads // nx * width), f32),
            pltpu.VMEM((batch, heads // nx * width), f32),
            pltpu.VMEM((chunks, ny, 2, batch, LANES), bf16),
            pltpu.VMEM((chunks, ny, 2, batch, LANES), bf16),
            pltpu.VMEM((batch, units), bf16),
            pltpu.VMEM((ychunks, nx, 2 * rows, ycols // 2), bf16),
            pltpu.VMEM((ychunks, nx, 2 * rows, ycols // 2), bf16),
            pltpu.VMEM((ychunks, batch, ycols), f32),
            sem, sem, sem((chunks,)), sem((chunks,)), sem((ychunks,)), sem((2,)),
            sem, sem, sem, sem, sem, sem, sem, sem,
            sem, sem((chunks,)), sem, sem, sem, sem((ychunks,)),
        ],
        compiler_params=pltpu.CompilerParams(
            collective_id=0, has_side_effects=True, vmem_limit_bytes=64 * 1024 * 1024 - 65536),
    )(
        residual,
        norm_gain,
        jnp.asarray(frequency).reshape(1, half),
        qkv_weight,
        out_weight,
        gate_weight,
        up_weight,
        down_weight,
        cache_keys,
        cache_values,
        lengths,
        positions,
    )


def fits_kernel(nx, ny, residual, qkv_weight, out_weight, gate_weight, cache_keys):
    rows, features = residual.shape
    own_rows, _, width = cache_keys.shape
    units = gate_weight.shape[1]
    held = features * (qkv_weight.shape[1] + 3 * units) + out_weight.size + 2 * cache_keys.size
    return (
        rows == 8
        and rows == own_rows * ny
        and width == 2 * LANES
        and qkv_weight.shape[1] % LANES == 0
        and out_weight.shape[0] % width == 0
        and units % (LANES * ny) == 0
        and units // (LANES * ny) >= 6
        and features % 512 == 0
        and 2 * held <= 58 * 1024 * 1024
    )


def shards(nx, ny, *operands):
    residual, _, qkv_weight, out_weight, gate_weight, _, _, cache_keys = operands[:8]
    if fits_kernel(nx, ny, residual, qkv_weight, out_weight, gate_weight, cache_keys):
        return kernel_shards(nx, ny, *operands)
    return collective_shards(*operands)


def solution(mesh):
    in_specs = (
        P(("groups", "gx"), "gy"),
        P("gy"),
        P("gy", "gx"),
        P("gx", "gy"),
        P("gy", "gx"),
        P("gy", "gx"),
        P("gx", "gy"),
        P(("groups", "gx", "gy"), None, None),
        P(("groups", "gx", "gy"), None, None),
        P(("groups", "gx", "gy")),
        P(("groups", "gx", "gy")),
    )
    out_specs = P(("groups", "gx"), "gy")
    body = functools.partial(shards, mesh.shape["gx"], mesh.shape["gy"])
    return jax.shard_map(body, mesh=mesh, in_specs=in_specs, out_specs=out_specs, check_vma=False)
```

```python
import functools

import jax
import jax.numpy as jnp
import numpy as np
from jax import lax
from jax.experimental import pallas as pl
from jax.experimental.pallas import tpu as pltpu
from jax.sharding import PartitionSpec as P

D = 8192
LANES = 128
MESH = pl.DeviceIdType.MESH


def angles(token_positions, head_width):
    half_width = head_width // 2
    frequency = jnp.exp(
        jnp.arange(half_width, dtype=jnp.float32) * (-2.0 * jnp.log(10000.0) / head_width)
    )
    return token_positions.astype(jnp.float32)[:, None] * frequency[None, :]


def rotary(vectors, turn):
    half_width = vectors.shape[-1] // 2
    first_half = vectors[..., :half_width]
    second_half = vectors[..., half_width:]
    cosine = jnp.cos(turn)
    sine_part = jnp.sin(turn)
    return jnp.concatenate(
        [
            first_half * cosine - second_half * sine_part,
            first_half * sine_part + second_half * cosine,
        ],
        axis=-1,
    )


def attend(joined, cached_keys, cached_values, valid_lengths, token_positions):
    row_count = joined.shape[0]
    head_width = cached_keys.shape[2]
    query_width = joined.shape[1] - 2 * head_width
    head_count = query_width // head_width
    queries = joined[:, :query_width].astype(jnp.float32).reshape(row_count, head_count, head_width)
    new_key = joined[:, query_width : query_width + head_width].astype(jnp.float32)
    new_value = joined[:, query_width + head_width :].astype(jnp.float32)
    turn = angles(token_positions, head_width)
    rotated_queries = rotary(queries, turn[:, None, :]).astype(jnp.bfloat16)
    rotated_key = rotary(new_key, turn).astype(jnp.bfloat16)
    score_scale = head_width ** (-0.5)
    scores = (
        jnp.einsum("rhd,rcd->rhc", rotated_queries, cached_keys, preferred_element_type=jnp.float32)
        * score_scale
    )
    visible = (
        jnp.arange(cached_keys.shape[1], dtype=jnp.int32)[None, None, :]
        < valid_lengths[:, None, None]
    )
    scores = jnp.where(visible, scores, -jnp.inf)
    own_score = (
        jnp.einsum("rhd,rd->rh", rotated_queries, rotated_key, preferred_element_type=jnp.float32)
        * score_scale
    )
    top_score = jnp.maximum(jnp.max(scores, axis=2), own_score)
    shifted = jnp.exp(scores - top_score[:, :, None])
    own_shifted = jnp.exp(own_score - top_score)
    denominator = jnp.sum(shifted, axis=2) + own_shifted
    softmax_weights = (shifted / denominator[:, :, None]).astype(jnp.bfloat16)
    own_weight = (own_shifted / denominator).astype(jnp.bfloat16)
    mixed = jnp.einsum(
        "rhc,rcd->rhd", softmax_weights, cached_values, preferred_element_type=jnp.float32
    )
    mixed = mixed + own_weight.astype(jnp.float32)[:, :, None] * new_value[:, None, :]
    return mixed.reshape(row_count, query_width).astype(jnp.bfloat16)


def collective_shards(
    residual,
    norm_gain,
    qkv_weight,
    out_weight,
    gate_weight,
    up_weight,
    down_weight,
    cache_keys,
    cache_values,
    lengths,
    positions,
):
    gain_wide = norm_gain.astype(jnp.float32)
    widened = residual.astype(jnp.float32)
    totals = lax.psum(jnp.sum(widened * widened, axis=1), "gy")
    scaled_rows = (widened * lax.rsqrt(totals / D + 1e-06)[:, None] * gain_wide).astype(
        jnp.bfloat16
    )
    normed = lax.all_gather(scaled_rows, "gx", axis=0, tiled=True)
    qkv_part = jnp.dot(normed, qkv_weight, preferred_element_type=jnp.float32)
    gate_part = jnp.dot(normed, gate_weight, preferred_element_type=jnp.float32)
    up_part = jnp.dot(normed, up_weight, preferred_element_type=jnp.float32)
    swapped = lax.all_to_all(qkv_part, "gx", split_axis=0, concat_axis=1, tiled=True)
    rows_qkv = lax.psum_scatter(swapped, "gy", scatter_dimension=0, tiled=True).astype(jnp.bfloat16)
    attended = attend(rows_qkv, cache_keys, cache_values, lengths, positions)
    grouped = lax.all_gather(attended, "gy", axis=0, tiled=True)
    heads_out = lax.all_to_all(grouped, "gx", split_axis=1, concat_axis=0, tiled=True)
    gate_sum, up_sum = lax.psum((gate_part, up_part), "gy")
    hidden = (jax.nn.silu(gate_sum) * up_sum).astype(jnp.bfloat16)
    block_term = jnp.dot(heads_out, out_weight, preferred_element_type=jnp.float32)
    return lax.psum_scatter(
        (block_term + jnp.dot(hidden, down_weight, preferred_element_type=jnp.float32)).astype(
            jnp.bfloat16
        ),
        "gx",
        scatter_dimension=0,
        tiled=True,
    )


def block_kernel(
    sizes,
    res_ref, gain_ref, freq_ref, qkv_hbm, out_hbm, gate_hbm, up_hbm, down_hbm, keys_hbm, vals_hbm,
    len_ref, pos_ref,
    y_ref,
    qkv_w, out_w, gate_w, up_w, down_w, keys_v, vals_v,
    res_send, res_all, ss_all, normed, q_send, q_all, qa, qc, att_send, att_all, att_x,
    gu_send, gu_all, hid, rs_send, rs_all, head_out,
    qkv_sem, out_sem, gate_sem, up_sem, down_sem, kv_sem,
    res_s, res_r, ss_s, ss_r, q_s, q_r, att_s, att_r, gu_s, gu_r, hid_s, hid_r, rs_s, rs_r,
):
    nx, ny = sizes["gx"], sizes["gy"]
    n = nx * ny
    g, i, j = lax.axis_index("groups"), lax.axis_index("gx"), lax.axis_index("gy")
    me = i * ny + j
    rows = res_ref.shape[0]
    own_rows = q_send.shape[1]
    half = res_ref.shape[1] // 2
    chunks, _, cols = gate_w.shape
    part = cols // ny
    ychunks, _, ycols = down_w.shape
    heads = qa.shape[1] - 8
    f32, bf16 = jnp.float32, jnp.bfloat16

    def peer(d):
        other = lax.rem(me + d, n)
        return (g, other // ny, lax.rem(other, ny)), other

    def gate_copy(c):
        return pltpu.make_async_copy(
            gate_hbm.at[:, pl.ds(pl.multiple_of(c * cols, cols), cols)], gate_w.at[c], gate_sem.at[c])

    def up_copy(c):
        return pltpu.make_async_copy(
            up_hbm.at[:, pl.ds(pl.multiple_of(c * cols, cols), cols)], up_w.at[c], up_sem.at[c])

    def down_copy(c):
        return pltpu.make_async_copy(
            down_hbm.at[:, pl.ds(pl.multiple_of(c * ycols, ycols), ycols)], down_w.at[c], down_sem.at[c])

    qkv_copy = pltpu.make_async_copy(qkv_hbm, qkv_w, qkv_sem)
    out_copy = pltpu.make_async_copy(out_hbm, out_w, out_sem)
    keys_copy = pltpu.make_async_copy(keys_hbm, keys_v, kv_sem.at[0])
    vals_copy = pltpu.make_async_copy(vals_hbm, vals_v, kv_sem.at[1])

    qkv_copy.start()
    keys_copy.start()
    vals_copy.start()

    def start_gu(c, carry):
        gate_copy(c).start()
        up_copy(c).start()
        return carry

    lax.fori_loop(0, chunks, start_gu, 0)
    out_copy.start()

    def start_down(c, carry):
        down_copy(c).start()
        return carry

    lax.fori_loop(0, ychunks, start_down, 0)

    barrier = pltpu.get_barrier_semaphore()

    def greet(d, carry):
        target, _ = peer(d)
        pl.semaphore_signal(barrier, inc=1, device_id=target, device_id_type=MESH)
        return carry

    lax.fori_loop(1, n, greet, 0)

    own = res_ref[...].astype(f32)
    packed = jnp.concatenate([own[:, :half], own[:, half:]], axis=0).astype(bf16)
    res_send[...] = packed
    res_all[i] = packed
    squares = jnp.sum(own * own, axis=1, keepdims=True)
    diagonal = lax.broadcasted_iota(jnp.int32, (rows, LANES), 0) == lax.broadcasted_iota(
        jnp.int32, (rows, LANES), 1)
    in_lanes = jnp.sum(jnp.where(diagonal, squares, 0.0), axis=0, keepdims=True)
    ss_all[me] = in_lanes

    pl.semaphore_wait(barrier, n - 1)

    def send_res(d, carry):
        to = lax.rem(i + d, nx)
        pltpu.make_async_remote_copy(
            src_ref=res_send, dst_ref=res_all.at[i], send_sem=res_s, recv_sem=res_r,
            device_id=(g, to, j), device_id_type=MESH).start()
        return carry

    def send_ss(d, carry):
        target, _ = peer(d)
        pltpu.make_async_remote_copy(
            src_ref=ss_all.at[me], dst_ref=ss_all.at[me], send_sem=ss_s, recv_sem=ss_r,
            device_id=target, device_id_type=MESH).start()
        return carry

    lax.fori_loop(1, nx, send_res, 0)
    lax.fori_loop(1, n, send_ss, 0)

    def drain(ref, sem):
        pltpu.make_async_copy(ref, ref, sem).wait()

    drain(ss_all.at[pl.ds(0, n - 1)], ss_r)
    drain(res_all.at[pl.ds(0, nx - 1)], res_r)

    gain = gain_ref[...].astype(f32).reshape(1, 2 * half)
    blocks = []
    for block in range(nx):
        lanes = ss_all[block * ny]
        for other in range(1, ny):
            lanes = lanes + ss_all[block * ny + other]
        total = jnp.sum(jnp.where(diagonal, lanes, 0.0), axis=1, keepdims=True)
        scale = lax.rsqrt(total / D + 1e-06)
        wide = res_all[block].astype(f32)
        wide = jnp.concatenate([wide[:rows], wide[rows:]], axis=1)
        blocks.append(wide * scale * gain)
    normed[...] = jnp.concatenate(blocks, axis=0).astype(bf16)

    qkv_copy.wait()
    qkv_part = jnp.dot(normed[...], qkv_w[...], preferred_element_type=f32)
    for to in range(n):
        q_send[to] = qkv_part[to * own_rows:(to + 1) * own_rows, :]
    q_all[me] = q_send[me]

    def send_q(d, carry):
        target, other = peer(d)
        pltpu.make_async_remote_copy(
            src_ref=q_send.at[other], dst_ref=q_all.at[me], send_sem=q_s, recv_sem=q_r,
            device_id=target, device_id_type=MESH).start()
        return carry

    lax.fori_loop(1, n, send_q, 0)

    def gu_step(c, carry):
        gate_copy(c).wait()
        gate = jnp.dot(normed[...], gate_w[c], preferred_element_type=f32).astype(bf16)
        for to in range(ny):
            gu_send[c, to, 0] = gate[:, to * part:(to + 1) * part]
        up_copy(c).wait()
        up = jnp.dot(normed[...], up_w[c], preferred_element_type=f32).astype(bf16)
        for to in range(ny):
            gu_send[c, to, 1] = up[:, to * part:(to + 1) * part]
        gu_all[c, j] = gu_send[c, j]

        def send_gu(d, inner):
            to = lax.rem(j + d, ny)
            pltpu.make_async_remote_copy(
                src_ref=gu_send.at[c, to], dst_ref=gu_all.at[c, j], send_sem=gu_s,
                recv_sem=gu_r.at[c], device_id=(g, i, to), device_id_type=MESH).start()
            return inner

        lax.fori_loop(1, ny, send_gu, 0)
        return carry

    def hid_step(c, carry):
        drain(gu_all.at[c, pl.ds(0, ny - 1)], gu_r.at[c])
        gate = gu_all[c, 0, 0].astype(f32)
        up = gu_all[c, 0, 1].astype(f32)
        for other in range(1, ny):
            gate = gate + gu_all[c, other, 0].astype(f32)
            up = up + gu_all[c, other, 1].astype(f32)
        here = hid.at[:, pl.ds(pl.multiple_of(c * cols + j * part, part), part)]
        here[...] = (gate / (1.0 + jnp.exp(-gate)) * up).astype(bf16)

        def send_hid(d, inner):
            to = lax.rem(j + d, ny)
            pltpu.make_async_remote_copy(
                src_ref=here, dst_ref=here, send_sem=hid_s, recv_sem=hid_r,
                device_id=(g, i, to), device_id_type=MESH).start()
            return inner

        lax.fori_loop(1, ny, send_hid, 0)
        return carry

    early = sizes["early"]
    lag = sizes["lag"]

    def both(c, carry):
        gu_step(c, 0)
        hid_step(c - lag, 0)
        return carry

    def run(first, end):
        middle = min(max(first, lag), end)
        lax.fori_loop(first, middle, gu_step, 0)
        lax.fori_loop(middle, end, both, 0)

    run(0, early)

    drain(q_all.at[pl.ds(0, n - 1)], q_r)
    per = q_all.shape[2] // LANES
    for block in range(nx):
        summed = q_all[block * ny]
        for other in range(1, ny):
            summed = summed + q_all[block * ny + other]
        summed = summed.astype(bf16).astype(f32)
        for at in range(per):
            index = block * per + at
            into = qa if index % 2 == 0 else qc
            for r in range(own_rows):
                into[r, index // 2:index // 2 + 1, :] = summed[r:r + 1, at * LANES:(at + 1) * LANES]
    keys_copy.wait()
    vals_copy.wait()
    context = keys_v.shape[1]
    score_scale = keys_v.shape[2] ** (-0.5)
    per_block = heads // nx
    for r in range(own_rows):
        turn = freq_ref[...] * pos_ref[r].astype(f32)
        cosine, sine = jnp.cos(turn), jnp.sin(turn)

        def rotated(a, c):
            return jnp.concatenate([a * cosine - c * sine, a * sine + c * cosine], axis=1).astype(bf16)

        queries = rotated(qa[r, 0:heads, :], qc[r, 0:heads, :])
        new_key = rotated(qa[r, heads:heads + 1, :], qc[r, heads:heads + 1, :])
        new_value = jnp.concatenate(
            [qa[r, heads + 1:heads + 2, :], qc[r, heads + 1:heads + 2, :]], axis=1)
        scores = lax.dot_general(
            queries, keys_v[r], (((1,), (1,)), ((), ())), preferred_element_type=f32) * score_scale
        visible = lax.broadcasted_iota(jnp.int32, (heads, context), 1) < len_ref[r]
        scores = jnp.where(visible, scores, -jnp.inf)
        own_score = jnp.sum(
            queries.astype(f32) * new_key.astype(f32), axis=1, keepdims=True) * score_scale
        top = jnp.maximum(jnp.max(scores, axis=1, keepdims=True), own_score)
        shifted = jnp.exp(scores - top)
        own_shifted = jnp.exp(own_score - top)
        total = jnp.sum(shifted, axis=1, keepdims=True) + own_shifted
        weights = (shifted / total).astype(bf16)
        own_weight = (own_shifted / total).astype(bf16).astype(f32)
        mixed = jnp.dot(weights, vals_v[r], preferred_element_type=f32) + own_weight * new_value
        mixed = mixed.astype(bf16).astype(f32)
        width = mixed.shape[1]
        for h in range(heads):
            at = h % per_block
            att_send[h // per_block, r:r + 1, at * width:(at + 1) * width] = mixed[h:h + 1, :]
    att_all[me] = att_send[i]

    def send_att(d, carry):
        target, other = peer(d)
        pltpu.make_async_remote_copy(
            src_ref=att_send.at[other // ny], dst_ref=att_all.at[me], send_sem=att_s,
            recv_sem=att_r, device_id=target, device_id_type=MESH).start()
        return carry

    lax.fori_loop(1, n, send_att, 0)

    run(early, chunks)
    lax.fori_loop(chunks - lag, chunks, hid_step, 0)

    drain(att_all.at[pl.ds(0, n - 1)], att_r)
    for source in range(n):
        att_x[source * own_rows:(source + 1) * own_rows, :] = att_all[source]
    out_copy.wait()
    attended = att_x[...].astype(bf16)

    def out_step(c, carry):
        at = pl.ds(pl.multiple_of(c * ycols, ycols), ycols)
        head_out[c] = jnp.dot(attended, out_w[:, at], preferred_element_type=f32)
        return carry

    lax.fori_loop(0, ychunks, out_step, 0)

    drain(hid.at[:, pl.ds(0, chunks * part * (ny - 1))], hid_r)

    def down_step(c, carry):
        down_copy(c).wait()
        term = head_out[c] + jnp.dot(hid[...], down_w[c], preferred_element_type=f32)
        for to in range(nx):
            mine = term[to * rows:(to + 1) * rows]
            rs_send[c, to] = jnp.concatenate(
                [mine[:, :ycols // 2], mine[:, ycols // 2:]], axis=0).astype(bf16)
        rs_all[c, i] = rs_send[c, i]

        def send_rs(d, inner):
            to = lax.rem(i + d, nx)
            pltpu.make_async_remote_copy(
                src_ref=rs_send.at[c, to], dst_ref=rs_all.at[c, i], send_sem=rs_s,
                recv_sem=rs_r.at[c], device_id=(g, to, j), device_id_type=MESH).start()
            return inner

        lax.fori_loop(1, nx, send_rs, 0)
        return carry

    lax.fori_loop(0, ychunks, down_step, 0)

    for c in range(ychunks):
        drain(rs_all.at[c, pl.ds(0, nx - 1)], rs_r.at[c])
        total = rs_all[c, 0].astype(f32)
        for other in range(1, nx):
            total = total + rs_all[c, other].astype(f32)
        y_ref[:, c * ycols:(c + 1) * ycols] = jnp.concatenate(
            [total[:rows], total[rows:]], axis=1).astype(bf16)

    def drain_res(d, carry):
        drain(res_send, res_s)
        return carry

    lax.fori_loop(1, nx, drain_res, 0)
    drain(ss_all.at[pl.ds(0, n - 1)], ss_s)
    drain(q_all.at[pl.ds(0, n - 1)], q_s)
    drain(att_all.at[pl.ds(0, n - 1)], att_s)
    drain(gu_all.at[:, pl.ds(0, ny - 1)], gu_s)
    drain(hid.at[:, pl.ds(0, chunks * part * (ny - 1))], hid_s)
    drain(rs_all.at[:, pl.ds(0, nx - 1)], rs_s)


def kernel_shards(
    nx,
    ny,
    residual,
    norm_gain,
    qkv_weight,
    out_weight,
    gate_weight,
    up_weight,
    down_weight,
    cache_keys,
    cache_values,
    lengths,
    positions,
):
    n = nx * ny
    rows, features = residual.shape
    own_rows, context, width = cache_keys.shape
    batch = rows * nx
    qkv_cols = qkv_weight.shape[1]
    heads = out_weight.shape[0] * nx // width
    units = gate_weight.shape[1]
    cols = LANES * ny
    chunks = units // cols
    ycols = 1024
    ychunks = features // ycols
    half = width // 2
    frequency = np.exp(np.arange(half) * (-2.0 * np.log(10000.0) / width)).astype(np.float32)
    f32, bf16 = jnp.float32, jnp.bfloat16
    sem = pltpu.SemaphoreType.DMA
    vmem = pl.BlockSpec(memory_space=pltpu.VMEM)
    smem = pl.BlockSpec(memory_space=pltpu.SMEM)
    hbm = pl.BlockSpec(memory_space=pl.ANY)
    sizes = {"gx": nx, "gy": ny, "early": min(7, chunks), "lag": min(6, chunks)}
    return pl.pallas_call(
        functools.partial(block_kernel, sizes),
        out_shape=jax.ShapeDtypeStruct((rows, features), bf16),
        in_specs=[vmem, vmem, vmem] + [hbm] * 7 + [smem, smem],
        out_specs=vmem,
        scratch_shapes=[
            pltpu.VMEM((features, qkv_cols), bf16),
            pltpu.VMEM(out_weight.shape, bf16),
            pltpu.VMEM((chunks, features, cols), bf16),
            pltpu.VMEM((chunks, features, cols), bf16),
            pltpu.VMEM((ychunks, units, ycols), bf16),
            pltpu.VMEM(cache_keys.shape, bf16),
            pltpu.VMEM(cache_values.shape, bf16),
            pltpu.VMEM((2 * rows, features // 2), bf16),
            pltpu.VMEM((nx, 2 * rows, features // 2), bf16),
            pltpu.VMEM((n, 1, LANES), f32),
            pltpu.VMEM((batch, features), bf16),
            pltpu.VMEM((n, own_rows, qkv_cols), f32),
            pltpu.VMEM((n, own_rows, qkv_cols), f32),
            pltpu.VMEM((own_rows, heads + 8, half), f32),
            pltpu.VMEM((own_rows, heads + 8, half), f32),
            pltpu.VMEM((nx, own_rows, heads // nx * width), f32),
            pltpu.VMEM((n, own_rows, heads // nx * width), f32),
            pltpu.VMEM((batch, heads // nx * width), f32),
            pltpu.VMEM((chunks, ny, 2, batch, LANES), bf16),
            pltpu.VMEM((chunks, ny, 2, batch, LANES), bf16),
            pltpu.VMEM((batch, units), bf16),
            pltpu.VMEM((ychunks, nx, 2 * rows, ycols // 2), bf16),
            pltpu.VMEM((ychunks, nx, 2 * rows, ycols // 2), bf16),
            pltpu.VMEM((ychunks, batch, ycols), f32),
            sem, sem, sem((chunks,)), sem((chunks,)), sem((ychunks,)), sem((2,)),
            sem, sem, sem, sem, sem, sem, sem, sem,
            sem, sem((chunks,)), sem, sem, sem, sem((ychunks,)),
        ],
        compiler_params=pltpu.CompilerParams(
            collective_id=0, has_side_effects=True, vmem_limit_bytes=64 * 1024 * 1024 - 65536),
    )(
        residual,
        norm_gain,
        jnp.asarray(frequency).reshape(1, half),
        qkv_weight,
        out_weight,
        gate_weight,
        up_weight,
        down_weight,
        cache_keys,
        cache_values,
        lengths,
        positions,
    )


def fits_kernel(nx, ny, residual, qkv_weight, out_weight, gate_weight, cache_keys):
    rows, features = residual.shape
    own_rows, _, width = cache_keys.shape
    units = gate_weight.shape[1]
    held = features * (qkv_weight.shape[1] + 3 * units) + out_weight.size + 2 * cache_keys.size
    return (
        rows == 8
        and rows == own_rows * ny
        and width == 2 * LANES
        and qkv_weight.shape[1] % LANES == 0
        and out_weight.shape[0] % width == 0
        and units % (LANES * ny) == 0
        and units // (LANES * ny) >= 6
        and features % 512 == 0
        and 2 * held <= 58 * 1024 * 1024
    )


def shards(nx, ny, *operands):
    residual, _, qkv_weight, out_weight, gate_weight, _, _, cache_keys = operands[:8]
    if fits_kernel(nx, ny, residual, qkv_weight, out_weight, gate_weight, cache_keys):
        return kernel_shards(nx, ny, *operands)
    return collective_shards(*operands)


def solution(mesh):
    in_specs = (
        P(("groups", "gx"), "gy"),
        P("gy"),
        P("gy", "gx"),
        P("gx", "gy"),
        P("gy", "gx"),
        P("gy", "gx"),
        P("gx", "gy"),
        P(("groups", "gx", "gy"), None, None),
        P(("groups", "gx", "gy"), None, None),
        P(("groups", "gx", "gy")),
        P(("groups", "gx", "gy")),
    )
    out_specs = P(("groups", "gx"), "gy")
    body = functools.partial(shards, mesh.shape["gx"], mesh.shape["gy"])
    return jax.shard_map(body, mesh=mesh, in_specs=in_specs, out_specs=out_specs, check_vma=False)
```
